128 devices in a mesh: node: 4 (over y), local: 32 (over x, z, core).
Axes of the slice: x: 4, y: 4, z: 4, core: 2. Of those that a mesh axis runs over, the one named last changes fastest.
Arguments:
- tokens: bfloat16 [16384, 7168], P(('node', 'local')), may hold values from -6 to 6
- route_ids: int32 [16384, 8], P(('node', 'local')), may hold values from 0 to 383, all different within a row; in each aligned block of 128 rows (0 to 127, 128 to 255, ...) at most 5 rows name the same one
- route_gates: bfloat16 [16384, 8], P(('node', 'local')), may hold values from 0.099609375 to 1
- limits: int32 [384], replicated, may hold values from 1 to 5, as said below
- w_gate: bfloat16 [128, 7168, 448], P(('node', 'local')), may hold values from -0.0625 to 0.0625
- w_up: bfloat16 [128, 7168, 448], P(('node', 'local')), may hold values from -0.0625 to 0.0625
- w_down: bfloat16 [128, 448, 7168], P(('node', 'local')), may hold values from -0.125 to 0.125
Outputs:
- mixed: bfloat16 [16384, 7168], P(('node', 'local'))
The draws below stay inside these ranges and needn't reach their ends.
Inputs may be any that keep to these rules, and one draw needn't show every extreme that they name: `route_ids`: in each aligned block of 128 rows (the rows of one device) no expert is named by more than 5 rows, a bound that some block reaches; a row names 8 different experts. `limits`: some expert's capacity is exactly 5.
All inputs are finite; a program needn't handle non-finite values.
Results may differ from the reference program's by a relative error of at most 0.0057.
Values may be sent and summed in bfloat16 or wider, within the bound.
No kernel may reach another device: no remote copies, remote signals or barrier semaphores. Data moves between devices by JAX's collectives and lax.ppermute only.
A program may use at most 128 MiB of HBM per device.

```python
import math
import jax
import jax.numpy as jnp
import numpy as np
from jax import lax

D = 7168
EXPERTS = 384
TOP = 8
FF_WIN = 1792
TOK_DEV = 128
GROUP = 4
CAP = 5
FF_SLAB = 448
EXP_HOST = 32
SLABS = 128
TOKENS = 16384


def draw_limits(key, part):
    key = jax.random.fold_in(key, 7)
    base_key, spot_key = jax.random.split(key)
    drawn = jax.random.randint(base_key, (EXPERTS,), 1, CAP + 1, dtype=jnp.int32)
    position = jax.random.randint(spot_key, (), 0, EXP_HOST, dtype=jnp.int32)
    return drawn.at[position].set(CAP)


def block_levels(rng, extent, cuts, least, largest):
    def one(dim, blocks):
        steps = jax.random.uniform(jax.random.fold_in(jax.random.fold_in(rng, 6), dim), (blocks,), jnp.float32, least / len(cuts), largest / len(cuts))
        return jnp.repeat(jnp.exp(steps), extent[dim] // blocks).reshape((-1,) + (1,) * (len(extent) - dim - 1))

    level = one(*cuts[0])
    for cut in cuts[1:]:
        level = level * one(*cut)
    return level


def shared_out(own_key, own, number, rows, count, top, bound, lean):
    ranking = jax.random.permutation(own_key, count)
    packed, usual = shares(count, rows * top, bound, lean, True), shares(count, rows * top, bound, lean, False)
    places = jnp.arange(count)

    def named(sizes, turn):
        used = int((sizes > 0).sum())
        fixed = max(1, used // 4)
        moved = fixed + (places - fixed + turn * (used - fixed)) % max(1, count - fixed)
        return jnp.zeros((count,), jnp.int32).at[ranking[jnp.where(places < fixed, places, moved)]].set(jnp.asarray(sizes, jnp.int32))

    sizes = jnp.where(number % 4 == 0, named(packed, number // 4), named(usual, number - number // 4 - 1))
    mixed = jax.random.permutation(jax.random.fold_in(own, 3), count)
    source_of, receiver = mixed[0:count // 2 * 2:2], mixed[1:count // 2 * 2:2]
    slack = jnp.minimum(sizes[source_of] - 1, bound - sizes[receiver]) // 2
    slack = jnp.where((source_of == ranking[0]) | (receiver == ranking[0]) | (sizes[receiver] == 0), 0, jnp.maximum(slack, 0))
    moved = jax.random.randint(jax.random.fold_in(own, 4), (count // 2,), 0, 1 << 20) % (slack + 1)
    sizes = sizes.at[source_of].add(-moved).at[receiver].add(moved)
    labels = jnp.searchsorted(jnp.cumsum(sizes), jnp.arange(rows * top), side="right").astype(jnp.int32)
    table = labels.reshape(top, rows).T
    table = table[jax.random.permutation(jax.random.fold_in(own, 1), rows)]
    turn = jax.random.randint(jax.random.fold_in(own, 2), (rows, 1), 0, top)
    return jnp.take_along_axis(table, (jnp.arange(top)[None, :] + turn) % top, axis=1)


def shares(number_of, total, limit, skew, full):
    weights = [(1 << 20) // math.isqrt(rank ** skew) + 1 for rank in range(1, number_of + 1)]
    largest = limit if full else min(limit, max(-(-total // number_of), total * weights[0] // sum(weights)))
    least = 1 if total - largest >= number_of - 1 else 0
    given, spare = [largest] + [least] * (number_of - 1), total - largest - least * (number_of - 1)
    while spare > 0:
        candidates = [i for i in range(1, number_of) if given[i] < largest] or [i for i in range(1, number_of) if given[i] < limit]
        mass, remaining = sum([weights[i] for i in candidates]), spare
        for i in candidates:
            addition = min(limit - given[i], max(1, remaining * weights[i] // mass), spare)
            given[i] = given[i] + addition
            spare = spare - addition
    return np.array(given)


def gaussian(stream_key, shape, deviation, limit, cuts=(), kind=jnp.bfloat16):
    result = jax.random.normal(stream_key, shape, jnp.float32) * deviation
    if len(cuts) > 0:
        result = block_levels(stream_key, shape, cuts, -0.22, 0.18) * result
    return jnp.clip(result, min=-limit, max=limit).astype(kind)


def setup_inputs(seed: int = 0) -> dict:
    arg_keys = jax.random.split(jax.random.key(seed), 8)
    tokens = gaussian(arg_keys[0], (TOKENS, D), 1.0, 6.0, ((0, 128),))
    route_ids_keys = jax.random.split(jax.random.fold_in(arg_keys[1], 1), TOKENS // TOK_DEV)
    route_ids_turns = jax.random.permutation(jax.random.fold_in(arg_keys[1], 3), TOKENS // TOK_DEV)
    route_ids = jax.vmap(lambda own, number: shared_out(jax.random.fold_in(arg_keys[1], 2), own, number, TOK_DEV, EXPERTS, TOP, CAP, 2))(route_ids_keys, route_ids_turns).reshape((TOKENS, TOP))
    route_gates = jnp.clip(jnp.exp(math.log(1.0) - 2.306499 * jax.random.uniform(arg_keys[2], (TOKENS, TOP), jnp.float32) ** block_levels(arg_keys[2], (TOKENS, TOP), ((0, 128),), -0.2, 0.2)), 0.099609375, 1.0).astype(jnp.bfloat16)
    limits = draw_limits(jax.random.fold_in(arg_keys[7], 71), 0)
    w_gate = gaussian(arg_keys[4], (SLABS, D, FF_SLAB), D ** -0.5, 0.0625, ((0, 128),))
    w_up = gaussian(arg_keys[5], (SLABS, D, FF_SLAB), D ** -0.5, 0.0625, ((0, 128),))
    w_down = gaussian(arg_keys[6], (SLABS, FF_SLAB, D), FF_WIN ** -0.5, 0.125, ((0, 128),))
    return dict(tokens=tokens, route_ids=route_ids, route_gates=route_gates, limits=limits, w_gate=w_gate, w_up=w_up, w_down=w_down)


def reference(tokens, route_ids, route_gates, limits, w_gate, w_up, w_down):
    blocks = TOKENS // TOK_DEV
    experts = jnp.arange(EXP_HOST, dtype=jnp.int32)
    matches = route_ids[:, :, None] == experts[None, None, :]
    per_tok = jnp.sum(matches.astype(jnp.int32), axis=1).astype(jnp.int32)
    per_block = per_tok.reshape(blocks, TOK_DEV, EXP_HOST)
    before = (jnp.cumsum(per_block, axis=1).astype(jnp.int32) - per_block).reshape(TOKENS, EXP_HOST)
    keep_mask = (per_tok > 0) & (before < limits[None, :EXP_HOST])
    gate_sum = jnp.sum(jnp.where(matches, route_gates.astype(jnp.float32)[:, :, None], jnp.float32(0.0)), axis=1)
    coef = jnp.where(keep_mask, gate_sum, jnp.float32(0.0))
    block_of = (jnp.arange(TOKENS, dtype=jnp.int32) // TOK_DEV).astype(jnp.int32)
    slot_of = jnp.where(keep_mask, block_of[:, None] * CAP + before, blocks * CAP).astype(jnp.int32)
    token_ids = jnp.broadcast_to(jnp.arange(TOKENS, dtype=jnp.int32)[:, None], (TOKENS, EXP_HOST))
    expert_ids = jnp.broadcast_to(experts[None, :], (TOKENS, EXP_HOST))
    row_index = jnp.zeros((EXP_HOST, blocks * CAP), jnp.int32).at[expert_ids, slot_of].set(token_ids, mode="drop")
    row_coef = jnp.zeros((EXP_HOST, blocks * CAP), jnp.float32).at[expert_ids, slot_of].set(coef, mode="drop")
    gate_all = w_gate.reshape(EXP_HOST, GROUP, D, FF_SLAB)
    up_all = w_up.reshape(EXP_HOST, GROUP, D, FF_SLAB)
    down_all = w_down.reshape(EXP_HOST, GROUP, FF_SLAB, D)

    def add_expert(total, pieces):
        gate_w, up_w, down_w, indices, coef_rows = pieces
        gathered = tokens[indices].astype(jnp.float32)
        gate_act = jnp.einsum("rd,sdf->srf", gathered, gate_w.astype(jnp.float32), precision=lax.Precision.HIGHEST)
        upper = jnp.einsum("rd,sdf->srf", gathered, up_w.astype(jnp.float32), precision=lax.Precision.HIGHEST)
        hidden = lax.optimization_barrier((jax.nn.silu(gate_act) * upper).astype(jnp.bfloat16))
        parts = jnp.einsum("srf,sfd->srd", hidden.astype(jnp.float32), down_w.astype(jnp.float32), precision=lax.Precision.HIGHEST)
        parts = lax.optimization_barrier(parts.astype(jnp.bfloat16))
        expert_out = jnp.sum(parts.astype(jnp.float32), axis=0)
        total = total.at[indices].add(coef_rows[:, None] * expert_out)
        return total, None

    total, _ = lax.scan(add_expert, jnp.zeros((TOKENS, D), jnp.float32), (gate_all, up_all, down_all, row_index, row_coef))
    return total.astype(jnp.bfloat16)
```

```python
import functools

import jax
import jax.numpy as jnp
from jax import lax
from jax.experimental import pallas as pl
from jax.experimental.pallas import tpu as pltpu
from jax.sharding import PartitionSpec as P

GROUP = 4
CAP = 5
LANE_BLOCKS = 8
BUNDLE = 32
PIECE = 64
BF16 = jnp.bfloat16
F32 = jnp.float32


def shuffle_matrix(to_rows):
    size = BUNDLE * LANE_BLOCKS
    out = lax.broadcasted_iota(jnp.int32, (size, size), 0)
    src = lax.broadcasted_iota(jnp.int32, (size, size), 1)
    if to_rows:
        want = (out & (LANE_BLOCKS - 1)) * BUNDLE + (out >> 3)
    else:
        want = (out & (BUNDLE - 1)) * LANE_BLOCKS + (out >> 5)
    return (src == want).astype(BF16)


def unpack_rows(shuffle, packed, rows_ref, g):
    part = packed.shape[1]
    flat = jnp.dot(shuffle, packed, preferred_element_type=F32).astype(BF16)
    at = pl.multiple_of(g * BUNDLE, BUNDLE)
    for b in range(LANE_BLOCKS):
        rows_ref[pl.ds(at, BUNDLE), b * part : (b + 1) * part] = flat[b * BUNDLE : (b + 1) * BUNDLE]


def pack_rows(shuffle, rows_ref, g):
    part = rows_ref.shape[1] // LANE_BLOCKS
    at = pl.multiple_of(g * BUNDLE, BUNDLE)
    stacked = jnp.concatenate(
        [rows_ref[pl.ds(at, BUNDLE), b * part : (b + 1) * part] for b in range(LANE_BLOCKS)], axis=0
    )
    return jnp.dot(shuffle, stacked, preferred_element_type=F32).astype(BF16)


def dispatch_kernel(limits_ref, ids_ref, gates_ref, tokens_ref, send_ref, coef_ref, rows_ref):
    toks = tokens_ref.shape[0]
    slots = rows_ref.shape[0]
    experts = slots // (2 * CAP)
    expert_at = lax.broadcasted_iota(jnp.int32, (experts, toks), 0)
    named = jnp.zeros((experts, toks), F32)
    gate = jnp.zeros((experts, toks), F32)
    for k in range(ids_ref.shape[0]):
        hit = ids_ref[k : k + 1, :] == expert_at
        named = named + jnp.where(hit, 1.0, 0.0)
        gate = gate + jnp.where(hit, gates_ref[k : k + 1, :].astype(F32), 0.0)
    earlier = (
        lax.broadcasted_iota(jnp.int32, (toks, toks), 0) < lax.broadcasted_iota(jnp.int32, (toks, toks), 1)
    ).astype(BF16)
    before = jnp.dot(named.astype(BF16), earlier, preferred_element_type=F32)
    capacity = jnp.zeros((experts, toks), F32)
    for e in range(experts):
        capacity = jnp.where(expert_at == e, limits_ref[e].astype(F32), capacity)
    kept = (named > 0) & (before < capacity)
    rank = jnp.where(kept, before + 1.0, 0.0)
    slot = lax.broadcasted_iota(jnp.int32, (slots, experts), 0)
    first = lax.broadcasted_iota(jnp.int32, (slots, experts), 1) * (2 * CAP)
    spread = ((slot >= first) & (slot < first + 2 * CAP)).astype(BF16)
    slot_rank = jnp.dot(spread, rank.astype(BF16), preferred_element_type=F32)
    slot_gate = jnp.dot(spread, gate.astype(BF16), preferred_element_type=F32)
    place = lax.rem(lax.broadcasted_iota(jnp.int32, (slots, toks), 0), CAP).astype(F32) + 1.0
    taken = slot_rank == place
    coef_ref[...] = jnp.where(taken, slot_gate, 0.0).T.astype(BF16)
    pick = jnp.where(taken, 1.0, 0.0).astype(BF16)
    width = tokens_ref.shape[1]
    step = 512

    @pl.loop(0, width // step)
    def _(j):
        at = pl.ds(pl.multiple_of(j * step, step), step)
        rows_ref[:, at] = jnp.dot(pick, tokens_ref[:, at], preferred_element_type=F32).astype(BF16)

    shuffle = shuffle_matrix(True)
    size = BUNDLE * LANE_BLOCKS

    @pl.loop(0, slots // BUNDLE)
    def _(g):
        send_ref[pl.ds(pl.multiple_of(g * size, size), size), :] = pack_rows(shuffle, rows_ref, g)


def experts_kernel(
    x_hbm, g0, g1, u0, u1, d0, d1, y_hbm, x_buf, rows_ref, w_buf, d_buf, acc_ref, x_sem, w_sem, d_sem, y_sem
):
    rows, width = rows_ref.shape
    slab = g0.shape[0]
    size = BUNDLE * LANE_BLOCKS
    bundles = rows // BUNDLE
    n_tile = 256
    per_tile = n_tile // PIECE
    tiles = 4 * slab // n_tile
    per_slab = slab // PIECE
    d_step = 512
    d_steps = width // d_step

    def x_copy(g):
        at = pl.ds(pl.multiple_of(g * size, size), size)
        return pltpu.make_async_copy(x_hbm.at[at, :], x_buf.at[at, :], x_sem.at[g])

    def y_copy(g):
        at = pl.ds(pl.multiple_of(g * size, size), size)
        return pltpu.make_async_copy(x_buf.at[at, :], y_hbm.at[at, :], y_sem.at[g])

    def w_copies(tile):
        copies = []
        for piece in range(tile * per_tile, (tile + 1) * per_tile):
            source = (g0, g1, u0, u1)[piece // per_slab]
            at = (piece % per_slab) * PIECE
            copies.append(
                pltpu.make_async_copy(
                    source.at[pl.ds(at, PIECE), :], w_buf.at[pl.ds(piece * PIECE, PIECE), :], w_sem.at[piece]
                )
            )
        return copies

    def d_copies(step):
        at = pl.ds(step * d_step, d_step)
        return [
            pltpu.make_async_copy(d.at[:, at], d_buf.at[pl.ds(i * slab, slab), at], d_sem.at[step, i])
            for i, d in enumerate((d0, d1))
        ]

    queue = [w_copies(i) for i in range(tiles)] + [d_copies(i) for i in range(d_steps)]
    ahead = 3

    def start(i):
        if i < len(queue):
            for copy in queue[i]:
                copy.start()

    for g in range(bundles):
        x_copy(g).start()
    for i in range(ahead):
        start(i)
    shuffle = shuffle_matrix(False)

    @pl.loop(0, bundles)
    def _(g):
        x_copy(g).wait()
        at = pl.ds(pl.multiple_of(g * size, size), size)
        unpack_rows(shuffle, x_buf[at, :], rows_ref, g)

    for tile in range(tiles):
        for copy in queue[tile]:
            copy.wait()
        start(tile + ahead)
        acc_ref[:, tile * n_tile : (tile + 1) * n_tile] = lax.dot_general(
            rows_ref[...],
            w_buf[tile * n_tile : (tile + 1) * n_tile, :],
            (((1,), (1,)), ((), ())),
            preferred_element_type=F32,
        )
    gate = acc_ref[:, : 2 * slab]
    hidden = (gate / (1.0 + jnp.exp(-gate)) * acc_ref[:, 2 * slab :]).astype(BF16)
    for step in range(d_steps):
        for copy in queue[tiles + step]:
            copy.wait()
        start(tiles + step + ahead)
        at = slice(step * d_step, (step + 1) * d_step)
        rows_ref[:, at] = jnp.dot(hidden, d_buf[:, at], preferred_element_type=F32).astype(BF16)
    back = shuffle_matrix(True)

    @pl.loop(0, bundles)
    def _(g):
        at = pl.ds(pl.multiple_of(g * size, size), size)
        x_buf[at, :] = pack_rows(back, rows_ref, g)
        y_copy(g).start()

    @pl.loop(0, bundles)
    def _(g):
        y_copy(g).wait()


def combine_kernel(coef_ref, y_ref, out_ref, rows_ref):
    size = BUNDLE * LANE_BLOCKS
    shuffle = shuffle_matrix(False)

    @pl.loop(0, rows_ref.shape[0] // BUNDLE)
    def _(g):
        at = pl.ds(pl.multiple_of(g * size, size), size)
        unpack_rows(shuffle, y_ref[at, :], rows_ref, g)

    step = 512

    @pl.loop(0, out_ref.shape[1] // step)
    def _(j):
        at = pl.ds(pl.multiple_of(j * step, step), step)
        out_ref[:, at] = jnp.dot(coef_ref[...], rows_ref[:, at], preferred_element_type=F32).astype(BF16)


def on_device(tokens, route_ids, route_gates, limits, w_gate, w_up, w_down):
    axes = ("node", "local")
    devices = lax.axis_size("node") * lax.axis_size("local")
    chips = devices // 2
    toks, width = tokens.shape
    slab = w_gate.shape[2]
    slots = chips * CAP
    part = width // LANE_BLOCKS
    vmem = pl.BlockSpec(memory_space=pltpu.VMEM)
    smem = pl.BlockSpec(memory_space=pltpu.SMEM)
    anywhere = pl.BlockSpec(memory_space=pl.ANY)
    limit = pltpu.CompilerParams(vmem_limit_bytes=60 * 1024 * 1024)

    gate_slab, up_slab, down_slab = w_gate[0].T, w_up[0].T, w_down[0]
    swap = [(i, i ^ 1) for i in range(devices)]
    with jax.named_scope("sibling_weights"):
        gate_other = lax.ppermute(gate_slab, axes, swap)
        up_other = lax.ppermute(up_slab, axes, swap)
        down_other = lax.ppermute(down_slab, axes, swap)

    send, coef = pl.pallas_call(
        dispatch_kernel,
        out_shape=(
            jax.ShapeDtypeStruct((slots * LANE_BLOCKS, part), BF16),
            jax.ShapeDtypeStruct((toks, slots), BF16),
        ),
        in_specs=[smem, vmem, vmem, vmem],
        out_specs=(vmem, vmem),
        scratch_shapes=[pltpu.VMEM((slots, width), BF16)],
        compiler_params=limit,
        name="dispatch",
    )(limits, route_ids.T, route_gates.T, tokens)

    same_core = [[2 * k + c for k in range(chips)] for c in range(2)]

    def exchange(rows):
        rows = rows.reshape(chips, CAP * LANE_BLOCKS, part)
        rows = lax.all_to_all(rows, axes, 0, 0, axis_index_groups=same_core, tiled=True)
        return rows.reshape(slots * LANE_BLOCKS, part)

    received = exchange(send)
    pieces = 4 * slab // PIECE
    bundles = slots // BUNDLE
    partial = pl.pallas_call(
        experts_kernel,
        out_shape=jax.ShapeDtypeStruct((slots * LANE_BLOCKS, part), BF16),
        in_specs=[anywhere] * 7,
        out_specs=anywhere,
        scratch_shapes=[
            pltpu.VMEM((slots * LANE_BLOCKS, part), BF16),
            pltpu.VMEM((slots, width), BF16),
            pltpu.VMEM((4 * slab, width), BF16),
            pltpu.VMEM((2 * slab, width), BF16),
            pltpu.VMEM((slots, 4 * slab), F32),
            pltpu.SemaphoreType.DMA((bundles,)),
            pltpu.SemaphoreType.DMA((pieces,)),
            pltpu.SemaphoreType.DMA((width // 512, 2)),
            pltpu.SemaphoreType.DMA((bundles,)),
        ],
        compiler_params=limit,
        name="experts",
    )(received, gate_slab, gate_other, up_slab, up_other, down_slab, down_other)

    returned = exchange(partial)
    return pl.pallas_call(
        combine_kernel,
        out_shape=jax.ShapeDtypeStruct((toks, width), BF16),
        in_specs=[vmem, vmem],
        out_specs=vmem,
        scratch_shapes=[pltpu.VMEM((slots, width), BF16)],
        compiler_params=limit,
        name="combine",
    )(coef, returned)


def solution(mesh):
    return jax.shard_map(
        on_device,
        mesh=mesh,
        in_specs=(
            P(("node", "local"), None),
            P(("node", "local"), None),
            P(("node", "local"), None),
            P(),
            P(("node", "local"), None, None),
            P(("node", "local"), None, None),
            P(("node", "local"), None, None),
        ),
        out_specs=P(("node", "local"), None),
        check_vma=False,
    )
```

```python
import jax
import jax.numpy as jnp
from jax import lax
from jax.experimental import pallas as pl
from jax.experimental.pallas import tpu as pltpu
from jax.sharding import PartitionSpec as P

GROUP = 4
CAP = 5
LANE_BLOCKS = 8
BUNDLE = 32
MIB = 1024 * 1024
BF16 = jnp.bfloat16
F32 = jnp.float32


def in_vmem(array):
    return pltpu.with_memory_space_constraint(array, pltpu.VMEM)


def in_hbm(array):
    return pltpu.with_memory_space_constraint(array, pltpu.HBM)


def shuffle_matrix(to_rows):
    size = BUNDLE * LANE_BLOCKS
    out = lax.broadcasted_iota(jnp.int32, (size, size), 0)
    src = lax.broadcasted_iota(jnp.int32, (size, size), 1)
    if to_rows:
        want = (out & (LANE_BLOCKS - 1)) * BUNDLE + (out >> 3)
    else:
        want = (out & (BUNDLE - 1)) * LANE_BLOCKS + (out >> 5)
    return (src == want).astype(BF16)


def unpack_rows(shuffle, packed, rows_ref, g):
    part = packed.shape[1]
    flat = jnp.dot(shuffle, packed, preferred_element_type=F32).astype(BF16)
    at = g * BUNDLE
    for b in range(LANE_BLOCKS):
        rows_ref[at : at + BUNDLE, b * part : (b + 1) * part] = flat[b * BUNDLE : (b + 1) * BUNDLE]


def pack_rows(shuffle, rows_ref, g):
    part = rows_ref.shape[1] // LANE_BLOCKS
    at = g * BUNDLE
    stacked = jnp.concatenate(
        [rows_ref[at : at + BUNDLE, b * part : (b + 1) * part] for b in range(LANE_BLOCKS)], axis=0
    )
    return jnp.dot(shuffle, stacked, preferred_element_type=F32).astype(BF16)


def dispatch_kernel(
    limits_ref, ids_ref, gates_ref, tokens_hbm, send_ref, coef_ref, tokens_ref, rows_ref, tokens_sem
):
    fetch = pltpu.make_async_copy(tokens_hbm, tokens_ref, tokens_sem)
    fetch.start()
    toks, width = tokens_ref.shape
    slots = rows_ref.shape[0]
    experts = slots // CAP
    expert_at = lax.broadcasted_iota(jnp.int32, (experts, toks), 0)
    named = jnp.zeros((experts, toks), F32)
    gate = jnp.zeros((experts, toks), F32)
    for k in range(ids_ref.shape[0]):
        hit = ids_ref[k : k + 1, :] == expert_at
        named = named + jnp.where(hit, 1.0, 0.0)
        gate = gate + jnp.where(hit, gates_ref[k : k + 1, :].astype(F32), 0.0)
    earlier = (
        lax.broadcasted_iota(jnp.int32, (toks, toks), 0) < lax.broadcasted_iota(jnp.int32, (toks, toks), 1)
    ).astype(BF16)
    before = jnp.dot(named.astype(BF16), earlier, preferred_element_type=F32)
    capacity = jnp.zeros((experts, toks), F32)
    for e in range(experts):
        capacity = jnp.where(expert_at == e, limits_ref[e].astype(F32), capacity)
    kept = (named > 0) & (before < capacity)
    rank = jnp.where(kept, before + 1.0, 0.0)
    slot = lax.broadcasted_iota(jnp.int32, (slots, experts), 0)
    first = lax.broadcasted_iota(jnp.int32, (slots, experts), 1) * CAP
    spread = ((slot >= first) & (slot < first + CAP)).astype(BF16)
    slot_rank = jnp.dot(spread, rank.astype(BF16), preferred_element_type=F32)
    slot_gate = jnp.dot(spread, gate.astype(BF16), preferred_element_type=F32)
    place = lax.rem(lax.broadcasted_iota(jnp.int32, (slots, toks), 0), CAP).astype(F32) + 1.0
    taken = slot_rank == place
    pick = jnp.where(taken, 1.0, 0.0).astype(BF16)
    fetch.wait()
    step = 1024
    for at in range(0, width, step):
        rows_ref[:, at : at + step] = jnp.dot(
            pick, tokens_ref[:, at : at + step], preferred_element_type=F32
        ).astype(BF16)
    shuffle = shuffle_matrix(True)
    size = BUNDLE * LANE_BLOCKS
    for g in range(slots // BUNDLE):
        packed = pack_rows(shuffle, rows_ref, g)
        for h in range(2):
            send_ref[h, g * size : (g + 1) * size, :] = packed
    coef_ref[...] = jnp.where(taken, slot_gate, 0.0).T.astype(BF16)


def experts_kernel(
    x_ref, g1, u1, d1, g0_hbm, u0_hbm, d0_hbm, y_ref, g0, u0, d0, rows_ref, hidden_ref, sem
):
    fetches = [
        pltpu.make_async_copy(source, place, sem.at[i])
        for i, (source, place) in enumerate(((g0_hbm, g0), (u0_hbm, u0), (d0_hbm, d0)))
    ]
    for fetch in fetches:
        fetch.start()
    rows, width = rows_ref.shape
    size = BUNDLE * LANE_BLOCKS
    bundles = rows // BUNDLE
    shuffle = shuffle_matrix(False)
    for g in range(bundles):
        unpack_rows(shuffle, x_ref[g * size : (g + 1) * size, :], rows_ref, g)
    across = (((1,), (1,)), ((), ()))

    def slab_hidden(gate_w, up_w):
        gate = lax.dot_general(rows_ref[...], gate_w[...], across, preferred_element_type=F32)
        upper = lax.dot_general(rows_ref[...], up_w[...], across, preferred_element_type=F32)
        return (gate / (1.0 + jnp.exp(-gate)) * upper).astype(BF16)

    hidden_ref[1] = slab_hidden(g1, u1)
    fetches[0].wait()
    fetches[1].wait()
    hidden_ref[0] = slab_hidden(g0, u0)
    fetches[2].wait()
    step = 1024
    for at in range(0, width, step):
        total = jnp.dot(hidden_ref[0], d0[:, at : at + step], preferred_element_type=F32)
        total += jnp.dot(hidden_ref[1], d1[:, at : at + step], preferred_element_type=F32)
        rows_ref[:, at : at + step] = total.astype(BF16)
    back = shuffle_matrix(True)
    for g in range(bundles):
        y_ref[g * size : (g + 1) * size, :] = pack_rows(back, rows_ref, g)


def combine_kernel(coef_ref, y_ref, out_hbm, out_ref, rows_ref, sem):
    size = BUNDLE * LANE_BLOCKS
    shuffle = shuffle_matrix(False)
    for g in range(rows_ref.shape[0] // BUNDLE):
        unpack_rows(shuffle, y_ref[g * size : (g + 1) * size, :], rows_ref, g)
    half = rows_ref.shape[0] // 2
    step = 1024
    copies = []
    for i, at in enumerate(range(0, out_ref.shape[1], step)):
        total = jnp.dot(coef_ref[...], rows_ref[:half, at : at + step], preferred_element_type=F32)
        total += jnp.dot(coef_ref[...], rows_ref[half:, at : at + step], preferred_element_type=F32)
        out_ref[:, at : at + step] = total.astype(BF16)
        columns = pl.ds(at, step)
        copies.append(pltpu.make_async_copy(out_ref.at[:, columns], out_hbm.at[:, columns], sem.at[i]))
        copies[-1].start()
    for copy in copies:
        copy.wait()


def on_device(tokens, route_ids, route_gates, limits, w_gate, w_up, w_down):
    axes = ("node", "local")
    devices = lax.axis_size("node") * lax.axis_size("local")
    chips = devices // 2
    hosted = chips // 2
    toks, width = tokens.shape
    slab = w_gate.shape[2]
    slots = hosted * CAP
    part = width // LANE_BLOCKS
    vmem = pl.BlockSpec(memory_space=pltpu.VMEM)
    smem = pl.BlockSpec(memory_space=pltpu.SMEM)
    anywhere = pl.BlockSpec(memory_space=pl.ANY)

    gate_slab, up_slab, down_slab = w_gate[0].T, w_up[0].T, w_down[0]
    swap = [(i, i ^ 1) for i in range(devices)]
    with jax.named_scope("sibling_weights"):
        gate_other = lax.ppermute(gate_slab, axes, swap)
        up_other = lax.ppermute(up_slab, axes, swap)
        down_other = lax.ppermute(down_slab, axes, swap)

    send, coef = pl.pallas_call(
        dispatch_kernel,
        out_shape=(
            pltpu.VMEM((2, slots * LANE_BLOCKS, part), BF16),
            pltpu.VMEM((toks, slots), BF16),
        ),
        in_specs=[smem, vmem, vmem, anywhere],
        out_specs=(vmem, vmem),
        scratch_shapes=[
            pltpu.VMEM((toks, width), BF16),
            pltpu.VMEM((slots, width), BF16),
            pltpu.SemaphoreType.DMA,
        ],
        compiler_params=pltpu.CompilerParams(vmem_limit_bytes=8 * MIB),
        name="dispatch",
    )(in_hbm(limits), in_hbm(route_ids.T), in_hbm(route_gates.T), in_hbm(tokens))

    order = [2 * (2 * e + h) for h in range(2) for e in range(hosted)]
    same_core = [[i + c for i in order] for c in range(2)]

    def exchange(rows):
        rows = rows.reshape(chips, CAP * LANE_BLOCKS, part)
        rows = lax.all_to_all(rows, axes, 0, 0, axis_index_groups=same_core, tiled=True)
        return rows.reshape(2 * slots * LANE_BLOCKS, part)

    received = exchange(send)
    slab_shapes = [pltpu.VMEM(w.shape, BF16) for w in (gate_slab, up_slab, down_slab)]
    partial = pl.pallas_call(
        experts_kernel,
        out_shape=pltpu.VMEM((2 * slots * LANE_BLOCKS, part), BF16),
        in_specs=[vmem] * 4 + [anywhere] * 3,
        out_specs=vmem,
        scratch_shapes=slab_shapes
        + [
            pltpu.VMEM((2 * slots, width), BF16),
            pltpu.VMEM((2, 2 * slots, slab), BF16),
            pltpu.SemaphoreType.DMA((3,)),
        ],
        compiler_params=pltpu.CompilerParams(vmem_limit_bytes=30 * MIB),
        name="experts",
    )(
        in_vmem(received),
        in_vmem(gate_other),
        in_vmem(up_other),
        in_vmem(down_other),
        in_hbm(gate_slab),
        in_hbm(up_slab),
        in_hbm(down_slab),
    )

    returned = exchange(partial)
    return pl.pallas_call(
        combine_kernel,
        out_shape=jax.ShapeDtypeStruct((toks, width), BF16),
        in_specs=[vmem, vmem],
        out_specs=anywhere,
        scratch_shapes=[
            pltpu.VMEM((toks, width), BF16),
            pltpu.VMEM((2 * slots, width), BF16),
            pltpu.SemaphoreType.DMA((width // 1024,)),
        ],
        compiler_params=pltpu.CompilerParams(vmem_limit_bytes=12 * MIB),
        name="combine",
    )(in_vmem(coef), in_vmem(returned))


def solution(mesh):
    return jax.shard_map(
        on_device,
        mesh=mesh,
        in_specs=(
            P(("node", "local"), None),
            P(("node", "local"), None),
            P(("node", "local"), None),
            P(),
            P(("node", "local"), None, None),
            P(("node", "local"), None, None),
            P(("node", "local"), None, None),
        ),
        out_specs=P(("node", "local"), None),
        check_vma=False,
    )
```

```python
import jax
import jax.numpy as jnp
from jax import lax
from jax.experimental import pallas as pl
from jax.experimental.pallas import tpu as pltpu
from jax.sharding import PartitionSpec as P

GROUP = 4
CAP = 5
LANE_BLOCKS = 8
BUNDLE = 32
MIB = 1024 * 1024
BF16 = jnp.bfloat16
F32 = jnp.float32


def in_vmem(array):
    return pltpu.with_memory_space_constraint(array, pltpu.VMEM)


def in_hbm(array):
    return pltpu.with_memory_space_constraint(array, pltpu.HBM)


def shuffle_matrix(to_rows):
    size = BUNDLE * LANE_BLOCKS
    out = lax.broadcasted_iota(jnp.int32, (size, size), 0)
    src = lax.broadcasted_iota(jnp.int32, (size, size), 1)
    if to_rows:
        want = (out & (LANE_BLOCKS - 1)) * BUNDLE + (out >> 3)
    else:
        want = (out & (BUNDLE - 1)) * LANE_BLOCKS + (out >> 5)
    return (src == want).astype(BF16)


def unpack_rows(shuffle, packed, rows_ref, g):
    part = packed.shape[1]
    flat = jnp.dot(shuffle, packed, preferred_element_type=F32).astype(BF16)
    at = g * BUNDLE
    for b in range(LANE_BLOCKS):
        rows_ref[at : at + BUNDLE, b * part : (b + 1) * part] = flat[b * BUNDLE : (b + 1) * BUNDLE]


def pack_rows(shuffle, rows_ref, g):
    part = rows_ref.shape[1] // LANE_BLOCKS
    at = g * BUNDLE
    stacked = jnp.concatenate(
        [rows_ref[at : at + BUNDLE, b * part : (b + 1) * part] for b in range(LANE_BLOCKS)], axis=0
    )
    return jnp.dot(shuffle, stacked, preferred_element_type=F32).astype(BF16)


def dispatch_kernel(
    limits_ref, ids_ref, gates_ref, tokens_hbm, send_ref, coef_ref, tokens_ref, rows_ref, tokens_sem
):
    fetch = pltpu.make_async_copy(tokens_hbm, tokens_ref, tokens_sem)
    fetch.start()
    toks, width = tokens_ref.shape
    slots = rows_ref.shape[0]
    experts = slots // CAP
    expert_at = lax.broadcasted_iota(jnp.int32, (experts, toks), 0)
    named = jnp.zeros((experts, toks), F32)
    gate = jnp.zeros((experts, toks), F32)
    for k in range(ids_ref.shape[0]):
        hit = ids_ref[k : k + 1, :] == expert_at
        named = named + jnp.where(hit, 1.0, 0.0)
        gate = gate + jnp.where(hit, gates_ref[k : k + 1, :].astype(F32), 0.0)
    earlier = (
        lax.broadcasted_iota(jnp.int32, (toks, toks), 0) < lax.broadcasted_iota(jnp.int32, (toks, toks), 1)
    ).astype(BF16)
    before = jnp.dot(named.astype(BF16), earlier, preferred_element_type=F32)
    capacity = jnp.zeros((experts, toks), F32)
    for e in range(experts):
        capacity = jnp.where(expert_at == e, limits_ref[e].astype(F32), capacity)
    kept = (named > 0) & (before < capacity)
    rank = jnp.where(kept, before + 1.0, 0.0)
    slot = lax.broadcasted_iota(jnp.int32, (slots, experts), 0)
    first = lax.broadcasted_iota(jnp.int32, (slots, experts), 1) * CAP
    spread = ((slot >= first) & (slot < first + CAP)).astype(BF16)
    slot_rank = jnp.dot(spread, rank.astype(BF16), preferred_element_type=F32)
    slot_gate = jnp.dot(spread, gate.astype(BF16), preferred_element_type=F32)
    place = lax.rem(lax.broadcasted_iota(jnp.int32, (slots, toks), 0), CAP).astype(F32) + 1.0
    taken = slot_rank == place
    pick = jnp.where(taken, 1.0, 0.0).astype(BF16)
    fetch.wait()
    step = 1024
    for at in range(0, width, step):
        rows_ref[:, at : at + step] = jnp.dot(
            pick, tokens_ref[:, at : at + step], preferred_element_type=F32
        ).astype(BF16)
    shuffle = shuffle_matrix(True)
    size = BUNDLE * LANE_BLOCKS
    for g in range(slots // BUNDLE):
        packed = pack_rows(shuffle, rows_ref, g)
        for h in range(2):
            send_ref[h, g * size : (g + 1) * size, :] = packed
    coef_ref[...] = jnp.where(taken, slot_gate, 0.0).T.astype(BF16)


def experts_kernel(x_ref, g0, u0, d0, g1, u1, d1, y_ref, rows_ref, hidden_ref):
    rows, width = rows_ref.shape
    size = BUNDLE * LANE_BLOCKS
    bundles = rows // BUNDLE
    shuffle = shuffle_matrix(False)
    for g in range(bundles):
        unpack_rows(shuffle, x_ref[g * size : (g + 1) * size, :], rows_ref, g)
    across = (((1,), (1,)), ((), ()))

    def slab_hidden(gate_w, up_w):
        gate = lax.dot_general(rows_ref[...], gate_w[...], across, preferred_element_type=F32)
        upper = lax.dot_general(rows_ref[...], up_w[...], across, preferred_element_type=F32)
        return (gate / (1.0 + jnp.exp(-gate)) * upper).astype(BF16)

    hidden_ref[0] = slab_hidden(g0, u0)
    hidden_ref[1] = slab_hidden(g1, u1)
    step = 1024
    for at in range(0, width, step):
        total = jnp.dot(hidden_ref[0], d0[:, at : at + step], preferred_element_type=F32)
        total += jnp.dot(hidden_ref[1], d1[:, at : at + step], preferred_element_type=F32)
        rows_ref[:, at : at + step] = total.astype(BF16)
    back = shuffle_matrix(True)
    for g in range(bundles):
        y_ref[g * size : (g + 1) * size, :] = pack_rows(back, rows_ref, g)


def combine_kernel(coef_ref, y_ref, out_hbm, out_ref, rows_ref, sem):
    size = BUNDLE * LANE_BLOCKS
    shuffle = shuffle_matrix(False)
    for g in range(rows_ref.shape[0] // BUNDLE):
        unpack_rows(shuffle, y_ref[g * size : (g + 1) * size, :], rows_ref, g)
    half = rows_ref.shape[0] // 2
    step = 1024
    copies = []
    for i, at in enumerate(range(0, out_ref.shape[1], step)):
        total = jnp.dot(coef_ref[...], rows_ref[:half, at : at + step], preferred_element_type=F32)
        total += jnp.dot(coef_ref[...], rows_ref[half:, at : at + step], preferred_element_type=F32)
        out_ref[:, at : at + step] = total.astype(BF16)
        columns = pl.ds(at, step)
        copies.append(pltpu.make_async_copy(out_ref.at[:, columns], out_hbm.at[:, columns], sem.at[i]))
        copies[-1].start()
    for copy in copies:
        copy.wait()


def on_device(tokens, route_ids, route_gates, limits, w_gate, w_up, w_down):
    axes = ("node", "local")
    devices = lax.axis_size("node") * lax.axis_size("local")
    chips = devices // 2
    hosted = chips // 2
    toks, width = tokens.shape
    slab = w_gate.shape[2]
    slots = hosted * CAP
    part = width // LANE_BLOCKS
    vmem = pl.BlockSpec(memory_space=pltpu.VMEM)
    smem = pl.BlockSpec(memory_space=pltpu.SMEM)
    anywhere = pl.BlockSpec(memory_space=pl.ANY)

    gate_slab, up_slab, down_slab = w_gate[0].T, w_up[0].T, w_down[0]
    swap = [(i, i ^ 1) for i in range(devices)]
    with jax.named_scope("sibling_weights"):
        gate_other = lax.ppermute(gate_slab, axes, swap)
        up_other = lax.ppermute(up_slab, axes, swap)
        down_other = lax.ppermute(down_slab, axes, swap)
        stay = [(i, i) for i in range(devices)]
        up_own = lax.ppermute(up_slab, axes, stay)
        down_own = lax.ppermute(down_slab, axes, stay)

    send, coef = pl.pallas_call(
        dispatch_kernel,
        out_shape=(
            pltpu.VMEM((2, slots * LANE_BLOCKS, part), BF16),
            pltpu.VMEM((toks, slots), BF16),
        ),
        in_specs=[smem, vmem, vmem, anywhere],
        out_specs=(vmem, vmem),
        scratch_shapes=[
            pltpu.VMEM((toks, width), BF16),
            pltpu.VMEM((slots, width), BF16),
            pltpu.SemaphoreType.DMA,
        ],
        compiler_params=pltpu.CompilerParams(vmem_limit_bytes=8 * MIB),
        name="dispatch",
    )(in_hbm(limits), in_hbm(route_ids.T), in_hbm(route_gates.T), in_hbm(tokens))

    order = [2 * (2 * e + h) for h in range(2) for e in range(hosted)]
    same_core = [[i + c for i in order] for c in range(2)]

    def exchange(rows):
        rows = rows.reshape(chips, CAP * LANE_BLOCKS, part)
        rows = lax.all_to_all(rows, axes, 0, 0, axis_index_groups=same_core, tiled=True)
        return rows.reshape(2 * slots * LANE_BLOCKS, part)

    received = exchange(send)
    partial = pl.pallas_call(
        experts_kernel,
        out_shape=pltpu.VMEM((2 * slots * LANE_BLOCKS, part), BF16),
        in_specs=[vmem] * 7,
        out_specs=vmem,
        scratch_shapes=[
            pltpu.VMEM((2 * slots, width), BF16),
            pltpu.VMEM((2, 2 * slots, slab), BF16),
        ],
        compiler_params=pltpu.CompilerParams(vmem_limit_bytes=11 * MIB),
        name="experts",
    )(
        in_vmem(received),
        in_vmem(gate_slab),
        in_vmem(up_own),
        in_vmem(down_own),
        in_vmem(gate_other),
        in_vmem(up_other),
        in_vmem(down_other),
    )

    returned = exchange(partial)
    return pl.pallas_call(
        combine_kernel,
        out_shape=jax.ShapeDtypeStruct((toks, width), BF16),
        in_specs=[vmem, vmem],
        out_specs=anywhere,
        scratch_shapes=[
            pltpu.VMEM((toks, width), BF16),
            pltpu.VMEM((2 * slots, width), BF16),
            pltpu.SemaphoreType.DMA((width // 1024,)),
        ],
        compiler_params=pltpu.CompilerParams(vmem_limit_bytes=12 * MIB),
        name="combine",
    )(in_vmem(coef), in_vmem(returned))


def solution(mesh):
    return jax.shard_map(
        on_device,
        mesh=mesh,
        in_specs=(
            P(("node", "local"), None),
            P(("node", "local"), None),
            P(("node", "local"), None),
            P(),
            P(("node", "local"), None, None),
            P(("node", "local"), None, None),
            P(("node", "local"), None, None),
        ),
        out_specs=P(("node", "local"), None),
        check_vma=False,
    )
```

```python
import jax
import jax.numpy as jnp
from jax import lax
from jax.experimental import pallas as pl
from jax.experimental.pallas import tpu as pltpu
from jax.sharding import PartitionSpec as P

GROUP = 4
CAP = 5
LANE_BLOCKS = 8
BUNDLE = 32
MIB = 1024 * 1024
BF16 = jnp.bfloat16
F32 = jnp.float32


def in_vmem(array):
    return pltpu.with_memory_space_constraint(array, pltpu.VMEM)


def in_hbm(array):
    return pltpu.with_memory_space_constraint(array, pltpu.HBM)


def shuffle_matrix(to_rows):
    size = BUNDLE * LANE_BLOCKS
    out = lax.broadcasted_iota(jnp.int32, (size, size), 0)
    src = lax.broadcasted_iota(jnp.int32, (size, size), 1)
    if to_rows:
        want = (out & (LANE_BLOCKS - 1)) * BUNDLE + (out >> 3)
    else:
        want = (out & (BUNDLE - 1)) * LANE_BLOCKS + (out >> 5)
    return (src == want).astype(BF16)


def unpack_rows(shuffle, packed, rows_ref, g):
    part = packed.shape[1]
    flat = jnp.dot(shuffle, packed, preferred_element_type=F32).astype(BF16)
    at = g * BUNDLE
    for b in range(LANE_BLOCKS):
        rows_ref[at : at + BUNDLE, b * part : (b + 1) * part] = flat[b * BUNDLE : (b + 1) * BUNDLE]


def pack_rows(shuffle, rows_ref, g):
    part = rows_ref.shape[1] // LANE_BLOCKS
    at = g * BUNDLE
    stacked = jnp.concatenate(
        [rows_ref[at : at + BUNDLE, b * part : (b + 1) * part] for b in range(LANE_BLOCKS)], axis=0
    )
    return jnp.dot(shuffle, stacked, preferred_element_type=F32).astype(BF16)


def dispatch_kernel(
    limits_ref, ids_ref, gates_ref, tokens_hbm, up_hbm, send_ref, coef_ref, up_ref, tokens_ref, rows_ref, sem
):
    fetch = pltpu.make_async_copy(tokens_hbm, tokens_ref, sem.at[0])
    fetch.start()
    fetch_up = pltpu.make_async_copy(up_hbm, up_ref, sem.at[1])
    fetch_up.start()
    toks, width = tokens_ref.shape
    slots = rows_ref.shape[0]
    experts = slots // CAP
    expert_at = lax.broadcasted_iota(jnp.int32, (experts, toks), 0)
    named = jnp.zeros((experts, toks), F32)
    gate = jnp.zeros((experts, toks), F32)
    for k in range(ids_ref.shape[0]):
        hit = ids_ref[k : k + 1, :] == expert_at
        named = named + jnp.where(hit, 1.0, 0.0)
        gate = gate + jnp.where(hit, gates_ref[k : k + 1, :].astype(F32), 0.0)
    earlier = (
        lax.broadcasted_iota(jnp.int32, (toks, toks), 0) < lax.broadcasted_iota(jnp.int32, (toks, toks), 1)
    ).astype(BF16)
    before = jnp.dot(named.astype(BF16), earlier, preferred_element_type=F32)
    capacity = jnp.zeros((experts, toks), F32)
    for e in range(experts):
        capacity = jnp.where(expert_at == e, limits_ref[e].astype(F32), capacity)
    kept = (named > 0) & (before < capacity)
    rank = jnp.where(kept, before + 1.0, 0.0)
    slot = lax.broadcasted_iota(jnp.int32, (slots, experts), 0)
    first = lax.broadcasted_iota(jnp.int32, (slots, experts), 1) * CAP
    spread = ((slot >= first) & (slot < first + CAP)).astype(BF16)
    slot_rank = jnp.dot(spread, rank.astype(BF16), preferred_element_type=F32)
    slot_gate = jnp.dot(spread, gate.astype(BF16), preferred_element_type=F32)
    place = lax.rem(lax.broadcasted_iota(jnp.int32, (slots, toks), 0), CAP).astype(F32) + 1.0
    taken = slot_rank == place
    pick = jnp.where(taken, 1.0, 0.0).astype(BF16)
    fetch.wait()
    step = 1024
    for at in range(0, width, step):
        rows_ref[:, at : at + step] = jnp.dot(
            pick, tokens_ref[:, at : at + step], preferred_element_type=F32
        ).astype(BF16)
    shuffle = shuffle_matrix(True)
    size = BUNDLE * LANE_BLOCKS
    for g in range(slots // BUNDLE):
        packed = pack_rows(shuffle, rows_ref, g)
        for h in range(2):
            send_ref[h, g * size : (g + 1) * size, :] = packed
    coef_ref[...] = jnp.where(taken, slot_gate, 0.0).T.astype(BF16)
    fetch_up.wait()


def experts_kernel(x_ref, g0, u0, d0, g1, u1, d1, y_ref, rows_ref, hidden_ref):
    rows, width = rows_ref.shape
    size = BUNDLE * LANE_BLOCKS
    bundles = rows // BUNDLE
    shuffle = shuffle_matrix(False)
    for g in range(bundles):
        unpack_rows(shuffle, x_ref[g * size : (g + 1) * size, :], rows_ref, g)
    across = (((1,), (1,)), ((), ()))

    def slab_hidden(gate_w, up_w):
        gate = lax.dot_general(rows_ref[...], gate_w[...], across, preferred_element_type=F32)
        upper = lax.dot_general(rows_ref[...], up_w[...], across, preferred_element_type=F32)
        return (gate / (1.0 + jnp.exp(-gate)) * upper).astype(BF16)

    hidden_ref[0] = slab_hidden(g0, u0)
    hidden_ref[1] = slab_hidden(g1, u1)
    step = 1024
    for at in range(0, width, step):
        total = jnp.dot(hidden_ref[0], d0[:, at : at + step], preferred_element_type=F32)
        total += jnp.dot(hidden_ref[1], d1[:, at : at + step], preferred_element_type=F32)
        rows_ref[:, at : at + step] = total.astype(BF16)
    back = shuffle_matrix(True)
    for g in range(bundles):
        y_ref[g * size : (g + 1) * size, :] = pack_rows(back, rows_ref, g)


def combine_kernel(coef_ref, y_ref, out_hbm, out_ref, rows_ref, sem):
    size = BUNDLE * LANE_BLOCKS
    shuffle = shuffle_matrix(False)
    for g in range(rows_ref.shape[0] // BUNDLE):
        unpack_rows(shuffle, y_ref[g * size : (g + 1) * size, :], rows_ref, g)
    half = rows_ref.shape[0] // 2
    step = 1024
    copies = []
    for i, at in enumerate(range(0, out_ref.shape[1], step)):
        total = jnp.dot(coef_ref[...], rows_ref[:half, at : at + step], preferred_element_type=F32)
        total += jnp.dot(coef_ref[...], rows_ref[half:, at : at + step], preferred_element_type=F32)
        out_ref[:, at : at + step] = total.astype(BF16)
        columns = pl.ds(at, step)
        copies.append(pltpu.make_async_copy(out_ref.at[:, columns], out_hbm.at[:, columns], sem.at[i]))
        copies[-1].start()
    for copy in copies:
        copy.wait()


def on_device(tokens, route_ids, route_gates, limits, w_gate, w_up, w_down):
    axes = ("node", "local")
    devices = lax.axis_size("node") * lax.axis_size("local")
    chips = devices // 2
    hosted = chips // 2
    toks, width = tokens.shape
    slab = w_gate.shape[2]
    slots = hosted * CAP
    part = width // LANE_BLOCKS
    vmem = pl.BlockSpec(memory_space=pltpu.VMEM)
    smem = pl.BlockSpec(memory_space=pltpu.SMEM)
    anywhere = pl.BlockSpec(memory_space=pl.ANY)

    gate_slab, up_slab, down_slab = w_gate[0].T, w_up[0].T, w_down[0]
    swap = [(i, i ^ 1) for i in range(devices)]
    with jax.named_scope("sibling_weights"):
        gate_other = lax.ppermute(gate_slab, axes, swap)
        up_other = lax.ppermute(up_slab, axes, swap)
        down_other = lax.ppermute(down_slab, axes, swap)

    send, coef, up_own = pl.pallas_call(
        dispatch_kernel,
        out_shape=(
            pltpu.VMEM((2, slots * LANE_BLOCKS, part), BF16),
            pltpu.VMEM((toks, slots), BF16),
            pltpu.VMEM((slab, width), BF16),
        ),
        in_specs=[smem, vmem, vmem, anywhere, anywhere],
        out_specs=(vmem, vmem, vmem),
        scratch_shapes=[
            pltpu.VMEM((toks, width), BF16),
            pltpu.VMEM((slots, width), BF16),
            pltpu.SemaphoreType.DMA((2,)),
        ],
        compiler_params=pltpu.CompilerParams(vmem_limit_bytes=8 * MIB),
        name="dispatch",
    )(in_hbm(limits), in_hbm(route_ids.T), in_hbm(route_gates.T), in_hbm(tokens), in_hbm(up_slab))

    order = [2 * (2 * e + h) for h in range(2) for e in range(hosted)]
    same_core = [[i + c for i in order] for c in range(2)]

    def exchange(rows):
        rows = rows.reshape(chips, CAP * LANE_BLOCKS, part)
        rows = lax.all_to_all(rows, axes, 0, 0, axis_index_groups=same_core, tiled=True)
        return rows.reshape(2 * slots * LANE_BLOCKS, part)

    received = exchange(send)
    partial = pl.pallas_call(
        experts_kernel,
        out_shape=pltpu.VMEM((2 * slots * LANE_BLOCKS, part), BF16),
        in_specs=[vmem] * 7,
        out_specs=vmem,
        scratch_shapes=[
            pltpu.VMEM((2 * slots, width), BF16),
            pltpu.VMEM((2, 2 * slots, slab), BF16),
        ],
        compiler_params=pltpu.CompilerParams(vmem_limit_bytes=11 * MIB),
        name="experts",
    )(
        in_vmem(received),
        in_vmem(gate_slab),
        in_vmem(up_own),
        in_vmem(down_slab),
        in_vmem(gate_other),
        in_vmem(up_other),
        in_vmem(down_other),
    )

    returned = exchange(partial)
    return pl.pallas_call(
        combine_kernel,
        out_shape=jax.ShapeDtypeStruct((toks, width), BF16),
        in_specs=[vmem, vmem],
        out_specs=anywhere,
        scratch_shapes=[
            pltpu.VMEM((toks, width), BF16),
            pltpu.VMEM((2 * slots, width), BF16),
            pltpu.SemaphoreType.DMA((width // 1024,)),
        ],
        compiler_params=pltpu.CompilerParams(vmem_limit_bytes=12 * MIB),
        name="combine",
    )(in_vmem(coef), in_vmem(returned))


def solution(mesh):
    return jax.shard_map(
        on_device,
        mesh=mesh,
        in_specs=(
            P(("node", "local"), None),
            P(("node", "local"), None),
            P(("node", "local"), None),
            P(),
            P(("node", "local"), None, None),
            P(("node", "local"), None, None),
            P(("node", "local"), None, None),
        ),
        out_specs=P(("node", "local"), None),
        check_vma=False,
    )
```

```python
import jax
import jax.numpy as jnp
from jax import lax
from jax.experimental import pallas as pl
from jax.experimental.pallas import tpu as pltpu
from jax.sharding import PartitionSpec as P

GROUP = 4
CAP = 5
LANE_BLOCKS = 8
BUNDLE = 32
MIB = 1024 * 1024
BF16 = jnp.bfloat16
F32 = jnp.float32


def in_vmem(array):
    return pltpu.with_memory_space_constraint(array, pltpu.VMEM)


def in_hbm(array):
    return pltpu.with_memory_space_constraint(array, pltpu.HBM)


def shuffle_matrix(to_rows):
    size = BUNDLE * LANE_BLOCKS
    out = lax.broadcasted_iota(jnp.int32, (size, size), 0)
    src = lax.broadcasted_iota(jnp.int32, (size, size), 1)
    if to_rows:
        want = (out & (LANE_BLOCKS - 1)) * BUNDLE + (out >> 3)
    else:
        want = (out & (BUNDLE - 1)) * LANE_BLOCKS + (out >> 5)
    return (src == want).astype(BF16)


def groups_of_two(count):
    return [range(g, min(g + 2, count)) for g in range(0, count, 2)]


def unpack_all(packed_ref, rows_ref):
    part = packed_ref.shape[1]
    size = BUNDLE * LANE_BLOCKS
    shuffle = shuffle_matrix(False)
    for group in groups_of_two(rows_ref.shape[0] // BUNDLE):
        packed = jnp.concatenate([packed_ref[g * size : (g + 1) * size, :] for g in group], axis=1)
        flat = jnp.dot(shuffle, packed, preferred_element_type=F32).astype(BF16)
        for i, g in enumerate(group):
            for b in range(LANE_BLOCKS):
                rows_ref[g * BUNDLE : (g + 1) * BUNDLE, b * part : (b + 1) * part] = flat[
                    b * BUNDLE : (b + 1) * BUNDLE, i * part : (i + 1) * part
                ]


def pack_all(rows_ref, store):
    part = rows_ref.shape[1] // LANE_BLOCKS
    size = BUNDLE * LANE_BLOCKS
    shuffle = shuffle_matrix(True)
    for group in groups_of_two(rows_ref.shape[0] // BUNDLE):
        stacked = [
            jnp.concatenate(
                [rows_ref[g * BUNDLE : (g + 1) * BUNDLE, b * part : (b + 1) * part] for b in range(LANE_BLOCKS)], axis=0
            )
            for g in group
        ]
        packed = jnp.dot(shuffle, jnp.concatenate(stacked, axis=1), preferred_element_type=F32).astype(BF16)
        for i, g in enumerate(group):
            store(slice(g * size, (g + 1) * size), packed[:, i * part : (i + 1) * part])


def dispatch_kernel(
    limits_ref, ids_ref, gates_ref, tokens_hbm, up_hbm, send_ref, coef_ref, up_ref, tokens_ref, rows_ref, sem
):
    fetch = pltpu.make_async_copy(tokens_hbm, tokens_ref, sem.at[0])
    fetch.start()
    fetch_up = pltpu.make_async_copy(up_hbm, up_ref, sem.at[1])
    fetch_up.start()
    toks, width = tokens_ref.shape
    slots = rows_ref.shape[0]
    experts = slots // CAP
    expert_at = lax.broadcasted_iota(jnp.int32, (experts, toks), 0)
    named = jnp.zeros((experts, toks), F32)
    gate = jnp.zeros((experts, toks), F32)
    for k in range(ids_ref.shape[0]):
        hit = ids_ref[k : k + 1, :] == expert_at
        named = named + jnp.where(hit, 1.0, 0.0)
        gate = gate + jnp.where(hit, gates_ref[k : k + 1, :].astype(F32), 0.0)
    earlier = (
        lax.broadcasted_iota(jnp.int32, (toks, toks), 0) < lax.broadcasted_iota(jnp.int32, (toks, toks), 1)
    ).astype(BF16)
    before = jnp.dot(named.astype(BF16), earlier, preferred_element_type=F32)
    capacity = jnp.zeros((experts, toks), F32)
    for e in range(experts):
        capacity = jnp.where(expert_at == e, limits_ref[e].astype(F32), capacity)
    kept = (named > 0) & (before < capacity)
    rank = jnp.where(kept, before + 1.0, 0.0)
    slot = lax.broadcasted_iota(jnp.int32, (slots, experts), 0)
    first = lax.broadcasted_iota(jnp.int32, (slots, experts), 1) * CAP
    spread = ((slot >= first) & (slot < first + CAP)).astype(BF16)
    slot_rank = jnp.dot(spread, rank.astype(BF16), preferred_element_type=F32)
    slot_gate = jnp.dot(spread, gate.astype(BF16), preferred_element_type=F32)
    place = lax.rem(lax.broadcasted_iota(jnp.int32, (slots, toks), 0), CAP).astype(F32) + 1.0
    taken = slot_rank == place
    pick = jnp.where(taken, 1.0, 0.0).astype(BF16)
    fetch.wait()
    step = 1024
    for at in range(0, width, step):
        rows_ref[:, at : at + step] = jnp.dot(
            pick, tokens_ref[:, at : at + step], preferred_element_type=F32
        ).astype(BF16)

    def store(at, packed):
        for h in range(2):
            send_ref[h, at, :] = packed

    pack_all(rows_ref, store)
    coef_ref[...] = jnp.where(taken, slot_gate, 0.0).T.astype(BF16)
    fetch_up.wait()


def experts_kernel(x_ref, g0, u0, d0, g1, u1, d1, y_ref, rows_ref, hidden_ref):
    width = rows_ref.shape[1]
    unpack_all(x_ref, rows_ref)
    across = (((1,), (1,)), ((), ()))

    def slab_hidden(gate_w, up_w):
        gate = lax.dot_general(rows_ref[...], gate_w[...], across, preferred_element_type=F32)
        upper = lax.dot_general(rows_ref[...], up_w[...], across, preferred_element_type=F32)
        return (gate / (1.0 + jnp.exp(-gate)) * upper).astype(BF16)

    hidden_ref[0] = slab_hidden(g0, u0)
    hidden_ref[1] = slab_hidden(g1, u1)
    step = 1024
    for at in range(0, width, step):
        total = jnp.dot(hidden_ref[0], d0[:, at : at + step], preferred_element_type=F32)
        total += jnp.dot(hidden_ref[1], d1[:, at : at + step], preferred_element_type=F32)
        rows_ref[:, at : at + step] = total.astype(BF16)

    def store(at, packed):
        y_ref[at, :] = packed

    pack_all(rows_ref, store)


def combine_kernel(coef_ref, y_ref, out_hbm, out_ref, rows_ref, sem):
    unpack_all(y_ref, rows_ref)
    half = rows_ref.shape[0] // 2
    step = 1024
    copies = []
    for i, at in enumerate(range(0, out_ref.shape[1], step)):
        total = jnp.dot(coef_ref[...], rows_ref[:half, at : at + step], preferred_element_type=F32)
        total += jnp.dot(coef_ref[...], rows_ref[half:, at : at + step], preferred_element_type=F32)
        out_ref[:, at : at + step] = total.astype(BF16)
        columns = pl.ds(at, step)
        copies.append(pltpu.make_async_copy(out_ref.at[:, columns], out_hbm.at[:, columns], sem.at[i]))
        copies[-1].start()
    for copy in copies:
        copy.wait()


def on_device(tokens, route_ids, route_gates, limits, w_gate, w_up, w_down):
    axes = ("node", "local")
    devices = lax.axis_size("node") * lax.axis_size("local")
    chips = devices // 2
    hosted = chips // 2
    toks, width = tokens.shape
    slab = w_gate.shape[2]
    slots = hosted * CAP
    part = width // LANE_BLOCKS
    vmem = pl.BlockSpec(memory_space=pltpu.VMEM)
    smem = pl.BlockSpec(memory_space=pltpu.SMEM)
    anywhere = pl.BlockSpec(memory_space=pl.ANY)

    gate_slab, up_slab, down_slab = w_gate[0].T, w_up[0].T, w_down[0]
    swap = [(i, i ^ 1) for i in range(devices)]
    with jax.named_scope("sibling_weights"):
        gate_other = lax.ppermute(gate_slab, axes, swap)
        up_other = lax.ppermute(up_slab, axes, swap)
        down_other = lax.ppermute(down_slab, axes, swap)

    send, coef, up_own = pl.pallas_call(
        dispatch_kernel,
        out_shape=(
            pltpu.VMEM((2, slots * LANE_BLOCKS, part), BF16),
            pltpu.VMEM((toks, slots), BF16),
            pltpu.VMEM((slab, width), BF16),
        ),
        in_specs=[smem, vmem, vmem, anywhere, anywhere],
        out_specs=(vmem, vmem, vmem),
        scratch_shapes=[
            pltpu.VMEM((toks, width), BF16),
            pltpu.VMEM((slots, width), BF16),
            pltpu.SemaphoreType.DMA((2,)),
        ],
        compiler_params=pltpu.CompilerParams(vmem_limit_bytes=8 * MIB),
        name="dispatch",
    )(in_hbm(limits), in_hbm(route_ids.T), in_hbm(route_gates.T), in_hbm(tokens), in_hbm(up_slab))

    order = [2 * (2 * e + h) for h in range(2) for e in range(hosted)]
    same_core = [[i + c for i in order] for c in range(2)]

    def exchange(rows):
        rows = rows.reshape(chips, CAP * LANE_BLOCKS, part)
        rows = lax.all_to_all(rows, axes, 0, 0, axis_index_groups=same_core, tiled=True)
        return rows.reshape(2 * slots * LANE_BLOCKS, part)

    received = exchange(send)
    partial = pl.pallas_call(
        experts_kernel,
        out_shape=pltpu.VMEM((2 * slots * LANE_BLOCKS, part), BF16),
        in_specs=[vmem] * 7,
        out_specs=vmem,
        scratch_shapes=[
            pltpu.VMEM((2 * slots, width), BF16),
            pltpu.VMEM((2, 2 * slots, slab), BF16),
        ],
        compiler_params=pltpu.CompilerParams(vmem_limit_bytes=11 * MIB),
        name="experts",
    )(
        in_vmem(received),
        in_vmem(gate_slab),
        in_vmem(up_own),
        in_vmem(down_slab),
        in_vmem(gate_other),
        in_vmem(up_other),
        in_vmem(down_other),
    )

    returned = exchange(partial)
    return pl.pallas_call(
        combine_kernel,
        out_shape=jax.ShapeDtypeStruct((toks, width), BF16),
        in_specs=[vmem, vmem],
        out_specs=anywhere,
        scratch_shapes=[
            pltpu.VMEM((toks, width), BF16),
            pltpu.VMEM((2 * slots, width), BF16),
            pltpu.SemaphoreType.DMA((width // 1024,)),
        ],
        compiler_params=pltpu.CompilerParams(vmem_limit_bytes=12 * MIB),
        name="combine",
    )(in_vmem(coef), in_vmem(returned))


def solution(mesh):
    return jax.shard_map(
        on_device,
        mesh=mesh,
        in_specs=(
            P(("node", "local"), None),
            P(("node", "local"), None),
            P(("node", "local"), None),
            P(),
            P(("node", "local"), None, None),
            P(("node", "local"), None, None),
            P(("node", "local"), None, None),
        ),
        out_specs=P(("node", "local"), None),
        check_vma=False,
    )
```

```python
import jax
import jax.numpy as jnp
from jax import lax
from jax.experimental import pallas as pl
from jax.experimental.pallas import tpu as pltpu
from jax.sharding import PartitionSpec as P

GROUP = 4
CAP = 5
LANE_BLOCKS = 8
BUNDLE = 32
MIB = 1024 * 1024
BF16 = jnp.bfloat16
F32 = jnp.float32


def in_vmem(array):
    return pltpu.with_memory_space_constraint(array, pltpu.VMEM)


def in_hbm(array):
    return pltpu.with_memory_space_constraint(array, pltpu.HBM)


def shuffle_matrix(to_rows):
    size = BUNDLE * LANE_BLOCKS
    out = lax.broadcasted_iota(jnp.int32, (size, size), 0)
    src = lax.broadcasted_iota(jnp.int32, (size, size), 1)
    if to_rows:
        want = (out & (LANE_BLOCKS - 1)) * BUNDLE + (out >> 3)
    else:
        want = (out & (BUNDLE - 1)) * LANE_BLOCKS + (out >> 5)
    return (src == want).astype(BF16)


def groups_of_two(count):
    return [range(g, min(g + 2, count)) for g in range(0, count, 2)]


def unpack_all(packed_ref, rows_ref):
    part = packed_ref.shape[1]
    size = BUNDLE * LANE_BLOCKS
    shuffle = shuffle_matrix(False)
    for group in groups_of_two(rows_ref.shape[0] // BUNDLE):
        packed = jnp.concatenate([packed_ref[g * size : (g + 1) * size, :] for g in group], axis=1)
        flat = jnp.dot(shuffle, packed, preferred_element_type=F32).astype(BF16)
        for i, g in enumerate(group):
            for b in range(LANE_BLOCKS):
                rows_ref[g * BUNDLE : (g + 1) * BUNDLE, b * part : (b + 1) * part] = flat[
                    b * BUNDLE : (b + 1) * BUNDLE, i * part : (i + 1) * part
                ]


def pack_all(rows_ref, store):
    part = rows_ref.shape[1] // LANE_BLOCKS
    size = BUNDLE * LANE_BLOCKS
    shuffle = shuffle_matrix(True)
    for group in groups_of_two(rows_ref.shape[0] // BUNDLE):
        stacked = [
            jnp.concatenate(
                [rows_ref[g * BUNDLE : (g + 1) * BUNDLE, b * part : (b + 1) * part] for b in range(LANE_BLOCKS)], axis=0
            )
            for g in group
        ]
        packed = jnp.dot(shuffle, jnp.concatenate(stacked, axis=1), preferred_element_type=F32).astype(BF16)
        for i, g in enumerate(group):
            store(slice(g * size, (g + 1) * size), packed[:, i * part : (i + 1) * part])


def dispatch_kernel(
    limits_hbm,
    ids_hbm,
    gates_hbm,
    tokens_hbm,
    up_hbm,
    send_ref,
    coef_ref,
    up_ref,
    limits_ref,
    ids_ref,
    gates_ref,
    tokens_ref,
    rows_ref,
    sem,
):
    fetches = [
        pltpu.make_async_copy(source, place, sem.at[i])
        for i, (source, place) in enumerate(
            (
                (ids_hbm, ids_ref),
                (gates_hbm, gates_ref),
                (limits_hbm, limits_ref),
                (tokens_hbm, tokens_ref),
                (up_hbm, up_ref),
            )
        )
    ]
    for fetch in fetches:
        fetch.start()
    for fetch in fetches[:3]:
        fetch.wait()
    toks, width = tokens_ref.shape
    slots = rows_ref.shape[0]
    experts = slots // CAP
    expert_at = lax.broadcasted_iota(jnp.int32, (experts, toks), 0)
    named = jnp.zeros((experts, toks), F32)
    gate = jnp.zeros((experts, toks), F32)
    for k in range(ids_ref.shape[0]):
        hit = ids_ref[k : k + 1, :] == expert_at
        named = named + jnp.where(hit, 1.0, 0.0)
        gate = gate + jnp.where(hit, gates_ref[k : k + 1, :].astype(F32), 0.0)
    earlier = (
        lax.broadcasted_iota(jnp.int32, (toks, toks), 0) < lax.broadcasted_iota(jnp.int32, (toks, toks), 1)
    ).astype(BF16)
    before = jnp.dot(named.astype(BF16), earlier, preferred_element_type=F32)
    capacity = jnp.zeros((experts, toks), F32)
    for e in range(experts):
        capacity = jnp.where(expert_at == e, limits_ref[e].astype(F32), capacity)
    kept = (named > 0) & (before < capacity)
    rank = jnp.where(kept, before + 1.0, 0.0)
    slot = lax.broadcasted_iota(jnp.int32, (slots, experts), 0)
    first = lax.broadcasted_iota(jnp.int32, (slots, experts), 1) * CAP
    spread = ((slot >= first) & (slot < first + CAP)).astype(BF16)
    slot_rank = jnp.dot(spread, rank.astype(BF16), preferred_element_type=F32)
    slot_gate = jnp.dot(spread, gate.astype(BF16), preferred_element_type=F32)
    place = lax.rem(lax.broadcasted_iota(jnp.int32, (slots, toks), 0), CAP).astype(F32) + 1.0
    taken = slot_rank == place
    pick = jnp.where(taken, 1.0, 0.0).astype(BF16)
    fetches[3].wait()
    step = 1024
    for at in range(0, width, step):
        rows_ref[:, at : at + step] = jnp.dot(
            pick, tokens_ref[:, at : at + step], preferred_element_type=F32
        ).astype(BF16)

    def store(at, packed):
        for h in range(2):
            send_ref[h, at, :] = packed

    pack_all(rows_ref, store)
    coef_ref[...] = jnp.where(taken, slot_gate, 0.0).T.astype(BF16)
    fetches[4].wait()


def experts_kernel(x_ref, g0, u0, d0, g1, u1, d1, y_ref, rows_ref, hidden_ref):
    width = rows_ref.shape[1]
    unpack_all(x_ref, rows_ref)
    across = (((1,), (1,)), ((), ()))

    def slab_hidden(gate_w, up_w):
        gate = lax.dot_general(rows_ref[...], gate_w[...], across, preferred_element_type=F32)
        upper = lax.dot_general(rows_ref[...], up_w[...], across, preferred_element_type=F32)
        return (gate / (1.0 + jnp.exp(-gate)) * upper).astype(BF16)

    hidden_ref[0] = slab_hidden(g0, u0)
    hidden_ref[1] = slab_hidden(g1, u1)
    step = 1024
    for at in range(0, width, step):
        total = jnp.dot(hidden_ref[0], d0[:, at : at + step], preferred_element_type=F32)
        total += jnp.dot(hidden_ref[1], d1[:, at : at + step], preferred_element_type=F32)
        rows_ref[:, at : at + step] = total.astype(BF16)

    def store(at, packed):
        y_ref[at, :] = packed

    pack_all(rows_ref, store)


def combine_kernel(coef_ref, y_ref, out_hbm, out_ref, rows_ref, sem):
    unpack_all(y_ref, rows_ref)
    half = rows_ref.shape[0] // 2
    step = 1024
    copies = []
    for i, at in enumerate(range(0, out_ref.shape[1], step)):
        total = jnp.dot(coef_ref[...], rows_ref[:half, at : at + step], preferred_element_type=F32)
        total += jnp.dot(coef_ref[...], rows_ref[half:, at : at + step], preferred_element_type=F32)
        out_ref[:, at : at + step] = total.astype(BF16)
        columns = pl.ds(at, step)
        copies.append(pltpu.make_async_copy(out_ref.at[:, columns], out_hbm.at[:, columns], sem.at[i]))
        copies[-1].start()
    for copy in copies:
        copy.wait()


def on_device(tokens, route_ids, route_gates, limits, w_gate, w_up, w_down):
    axes = ("node", "local")
    devices = lax.axis_size("node") * lax.axis_size("local")
    chips = devices // 2
    hosted = chips // 2
    toks, width = tokens.shape
    slab = w_gate.shape[2]
    slots = hosted * CAP
    part = width // LANE_BLOCKS
    vmem = pl.BlockSpec(memory_space=pltpu.VMEM)
    anywhere = pl.BlockSpec(memory_space=pl.ANY)

    gate_slab, up_slab, down_slab = w_gate[0].T, w_up[0].T, w_down[0]
    swap = [(i, i ^ 1) for i in range(devices)]
    with jax.named_scope("sibling_weights"):
        gate_other = lax.ppermute(gate_slab, axes, swap)
        up_other = lax.ppermute(up_slab, axes, swap)
        down_other = lax.ppermute(down_slab, axes, swap)

    send, coef, up_own = pl.pallas_call(
        dispatch_kernel,
        out_shape=(
            pltpu.VMEM((2, slots * LANE_BLOCKS, part), BF16),
            pltpu.VMEM((toks, slots), BF16),
            pltpu.VMEM((slab, width), BF16),
        ),
        in_specs=[anywhere] * 5,
        out_specs=(vmem, vmem, vmem),
        scratch_shapes=[
            pltpu.SMEM(limits.shape, jnp.int32),
            pltpu.VMEM(route_ids.shape[::-1], jnp.int32),
            pltpu.VMEM(route_gates.shape[::-1], BF16),
            pltpu.VMEM((toks, width), BF16),
            pltpu.VMEM((slots, width), BF16),
            pltpu.SemaphoreType.DMA((5,)),
        ],
        compiler_params=pltpu.CompilerParams(vmem_limit_bytes=8 * MIB),
        name="dispatch",
    )(in_hbm(limits), in_hbm(route_ids.T), in_hbm(route_gates.T), in_hbm(tokens), in_hbm(up_slab))

    order = [2 * (2 * e + h) for h in range(2) for e in range(hosted)]
    same_core = [[i + c for i in order] for c in range(2)]

    def exchange(rows):
        rows = rows.reshape(chips, CAP * LANE_BLOCKS, part)
        rows = lax.all_to_all(rows, axes, 0, 0, axis_index_groups=same_core, tiled=True)
        return rows.reshape(2 * slots * LANE_BLOCKS, part)

    received = exchange(send)
    partial = pl.pallas_call(
        experts_kernel,
        out_shape=pltpu.VMEM((2 * slots * LANE_BLOCKS, part), BF16),
        in_specs=[vmem] * 7,
        out_specs=vmem,
        scratch_shapes=[
            pltpu.VMEM((2 * slots, width), BF16),
            pltpu.VMEM((2, 2 * slots, slab), BF16),
        ],
        compiler_params=pltpu.CompilerParams(vmem_limit_bytes=11 * MIB),
        name="experts",
    )(
        in_vmem(received),
        in_vmem(gate_slab),
        in_vmem(up_own),
        in_vmem(down_slab),
        in_vmem(gate_other),
        in_vmem(up_other),
        in_vmem(down_other),
    )

    returned = exchange(partial)
    return pl.pallas_call(
        combine_kernel,
        out_shape=jax.ShapeDtypeStruct((toks, width), BF16),
        in_specs=[vmem, vmem],
        out_specs=anywhere,
        scratch_shapes=[
            pltpu.VMEM((toks, width), BF16),
            pltpu.VMEM((2 * slots, width), BF16),
            pltpu.SemaphoreType.DMA((width // 1024,)),
        ],
        compiler_params=pltpu.CompilerParams(vmem_limit_bytes=12 * MIB),
        name="combine",
    )(in_vmem(coef), in_vmem(returned))


def solution(mesh):
    return jax.shard_map(
        on_device,
        mesh=mesh,
        in_specs=(
            P(("node", "local"), None),
            P(("node", "local"), None),
            P(("node", "local"), None),
            P(),
            P(("node", "local"), None, None),
            P(("node", "local"), None, None),
            P(("node", "local"), None, None),
        ),
        out_specs=P(("node", "local"), None),
        check_vma=False,
    )
```
